32 devices in a mesh: grp: 1, row: 4 (over z), col: 4 (over y, x), layer: 2 (over core).
Axes of the slice: x: 2, y: 2, z: 4, core: 2. Of those that a mesh axis runs over, the one named last changes fastest.
Arguments:
- a_blocks: bfloat16 [4, 2, 4, 6, 128, 128], P(('grp', 'row'), 'layer', 'col'), may hold values from -6 to 6
- a_rows: int32 [4, 2, 4, 6], P(('grp', 'row'), 'layer', 'col'), may hold values from 0 to 15, all different within a row
- b_blocks: bfloat16 [4, 2, 128, 1024], P(('grp', 'col'), 'layer', None, 'row'), may hold values from -0.5 to 0.5
- b_occupied: int32 [4, 2, 8], P(('grp', 'col'), 'layer', 'row'), may hold values 0 or 1
- keep: int32 [64, 8], P(('grp', 'col'), 'row'), may hold values 0 or 1
- owner_rows: int32 [4, 2, 8], P(('grp', 'col')), may hold values from 0 to 7, each once within a row
Outputs:
- owned: bfloat16 [8, 8, 128, 1024], P(('grp', 'col', 'layer'), None, None, 'row')
The draws below stay inside these ranges and needn't reach their ends.
Inputs may be any that keep to these rules, and one draw needn't show every extreme that they name: `a_rows`: the 6 numbers of one list are different. `owner_rows`: each list over the last dimension names every number once.
All inputs are finite; a program needn't handle non-finite values. No bound on the sum of `b_occupied` or of `keep` on one device may be relied on, other than what follows from the above.
Results may differ from the reference program's by a relative error of at most 0.001.
Values may be sent and summed in bfloat16 or wider, within the bound.
No kernel may reach another device: no remote copies, remote signals or barrier semaphores. Data moves between devices by JAX's collectives and lax.ppermute only.
A program may use at most 64 MiB of HBM per device.

```python
import jax
import jax.numpy as jnp
from jax import lax

BS = 128
OCCA = 6
NB = 8
OWN = 8
MBC = 16
MB = 64
N_COL = 4
N_LAYER = 2


def place_ends(result, own_key, smallest, top_value):
    place = [jax.random.randint(jax.random.fold_in(own_key, axis), (), 0, length) for axis, length in enumerate(result.shape)]
    longest = result.shape.index(max(result.shape))
    neighbour = place[:longest] + [(place[longest] + 1) % result.shape[longest]] + place[longest + 1:]
    return result.at[tuple(place)].set(smallest).at[tuple(neighbour)].set(top_value)


def shard_levels(rng, dims, split, least, largest):
    factor_of, own = 1.0, jax.random.fold_in(rng, 6)
    for dim, parts in split:
        heights = jnp.exp(jax.random.uniform(jax.random.fold_in(own, dim), (parts,), jnp.float32, least / len(split), largest / len(split)))
        factor_of = factor_of * jnp.repeat(heights, dims[dim] // parts).reshape([-1 if axis == dim else 1 for axis in range(len(dims))])
    return factor_of


def different_ones(key, rows, amount, top, lift):
    order = jax.random.permutation(jax.random.fold_in(key, 1), amount)
    pull = order
    for power in range(3):
        pull = pull * pull // amount
    pull = pull * lift // amount
    tickets = jax.random.randint(jax.random.fold_in(key, 2), (rows, amount), 0, 4096) + pull
    holders = jax.random.permutation(jax.random.fold_in(key, 3), rows)[jnp.arange(amount) % rows]
    tickets = jnp.where(jnp.arange(rows)[:, None] == holders[None, :], 1 << 14, tickets)
    priority = tickets * amount + jnp.arange(amount)
    return lax.top_k(priority.astype(jnp.int32), top)[1].astype(jnp.int32)


def normal_values(stream_key, dims, scale, reach, split=(), kind=jnp.bfloat16):
    gain = shard_levels(stream_key, dims, split, -0.22, 0.18) if split else 1.0
    drawn = jax.random.normal(stream_key, dims, jnp.float32) * scale * gain
    return jnp.minimum(jnp.maximum(drawn, -reach), reach).astype(kind)


def setup_inputs(seed: int = 0, part: int = 0) -> dict:
    keys = jax.random.split(jax.random.key(seed), 7)
    own_keys = jax.random.split(jax.random.fold_in(keys[6], part), 7)
    a_blocks = normal_values(own_keys[0], (NB // N_LAYER, N_LAYER, N_COL, OCCA, BS, BS), 1.0, 6.0, ((0, 4), (1, 2), (2, 4)))
    a_rows = different_ones(own_keys[1], (NB // N_LAYER) * N_LAYER * N_COL, MBC, OCCA, 0).reshape((NB // N_LAYER, N_LAYER, N_COL, OCCA))
    b_blocks = normal_values(own_keys[2], (NB // N_LAYER, N_LAYER, BS, NB * BS), (BS * NB // 8) ** -0.5, 0.5, ((0, 4), (1, 2), (3, 4)))
    b_occupied = place_ends((jax.random.randint(own_keys[3], (NB // N_LAYER, N_LAYER, NB), 0, 5) < 2).astype(jnp.int32), jax.random.fold_in(own_keys[3], 1), 0, 1)
    keep = place_ends((jax.random.randint(own_keys[4], (MB, NB), 0, 2) < 1).astype(jnp.int32), jax.random.fold_in(own_keys[4], 1), 0, 1)
    owner_rows = jax.vmap(lambda own: jax.random.permutation(own, OWN))(jax.random.split(own_keys[5], N_COL * N_LAYER)).reshape((N_COL, N_LAYER, OWN)).astype(jnp.int32)
    return {"a_blocks": a_blocks, "a_rows": a_rows, "b_blocks": b_blocks, "b_occupied": b_occupied, "keep": keep, "owner_rows": owner_rows}


def reference(a_blocks, a_rows, b_blocks, b_occupied, keep, owner_rows):
    matrix_order = NB * BS
    values = a_blocks.reshape(NB, N_COL * OCCA, BS, BS)
    offsets = (jnp.arange(N_COL, dtype=jnp.int32) * MBC)[None, :, None]
    global_rows = (a_rows.reshape(NB, N_COL, OCCA) + offsets).reshape(NB, N_COL * OCCA).astype(jnp.int32)
    occupied = b_occupied.reshape(NB, 1, NB, 1).astype(b_blocks.dtype)
    panel_rows = (b_blocks.reshape(NB, BS, NB, BS) * occupied).reshape(NB, BS, matrix_order)

    def accumulate(running, inputs):
        block_values, block_rows, panel_row = inputs
        partial_value = jnp.einsum("sab,bc->sac", block_values.astype(jnp.float32), panel_row.astype(jnp.float32), precision=lax.Precision.HIGHEST)
        return running.at[block_rows].add(partial_value), None

    start_value = jnp.zeros((MB, BS, matrix_order), jnp.float32)
    product = lax.scan(accumulate, start_value, (values, global_rows, panel_rows))[0]
    kept_mask = keep.reshape(MB, 1, NB, 1).astype(jnp.float32)
    filtered = (product.reshape(MB, BS, NB, BS) * kept_mask).reshape(MB, BS, matrix_order)
    half_rows = MBC // N_LAYER
    picked = (jnp.arange(N_COL, dtype=jnp.int32)[:, None, None] * MBC
              + jnp.arange(N_LAYER, dtype=jnp.int32)[None, :, None] * half_rows
              + owner_rows.astype(jnp.int32))
    picked = jnp.transpose(picked, (2, 0, 1)).reshape(OWN, N_COL * N_LAYER)
    return filtered[picked].astype(jnp.bfloat16)
```

```python
import functools

import jax
import jax.numpy as jnp
from jax import lax
from jax.experimental import pallas as pl
from jax.experimental.pallas import tpu as pltpu
from jax.sharding import PartitionSpec as P


def product_kernel(orders, place_ref, ids_ref, owner_ref, keep_ref, b_ref, *refs):
    piece_refs = refs[: len(orders)]
    out_ref, table, panels = refs[len(orders) :]
    row, layer = place_ref[0], place_ref[1]
    row_count, layer_count, slot_count = ids_ref.shape
    half_rows, group_rows = owner_ref.shape[1], keep_ref.shape[0]
    local_rows = b_ref.shape[2]
    block_size = b_ref.shape[3]
    out_count = out_ref.shape[0]
    own_cols = out_count // layer_count
    steps = []
    for ref, order in zip(piece_refs, orders):
        for at, (flip_row, flip_layer) in enumerate(order):
            steps.append((ref, at, row ^ flip_row, flip_layer))
    places = []
    for ref, at, i, flip_layer in steps:
        places.append((i, layer ^ flip_layer))
    for n, (i, which) in enumerate(places):
        for m in range(group_rows):
            table[n, m] = -1
    for n, (i, which) in enumerate(places):
        for s in range(slot_count):
            table[n, ids_ref[i, which, s]] = s
    for n, (i, which) in enumerate(places):
        panels[n * block_size : (n + 1) * block_size, :] = b_ref[i // local_rows, which, i % local_rows]
    lane = lax.broadcasted_iota(jnp.int32, (1, b_ref.shape[4]), 1)
    for q in range(out_count):
        owner, half = q // layer_count, q % layer_count
        m = half * half_rows + owner_ref[half, owner * layer_count + layer]
        parts = []
        for n, (ref, at, _, _) in enumerate(steps):
            s = table[n, m]
            block = ref[at, jnp.maximum(s, 0)]
            parts.append(jnp.where(s >= 0, block, jnp.zeros_like(block)))
        total = jnp.dot(jnp.concatenate(parts, axis=1), panels[...], preferred_element_type=jnp.float32)
        kept = jnp.zeros((1, b_ref.shape[4]), jnp.float32)
        for n in range(keep_ref.shape[1]):
            kept = jnp.where(lane // block_size == n, keep_ref[m, n].astype(jnp.float32), kept)
        out_ref[q] = (total * kept).astype(out_ref.dtype)


def product(place, ids, owner_rows, keep, panels, pieces, orders):
    layer_count = ids.shape[1]
    block_size, width = panels.shape[3:]
    step_count = sum(len(order) for order in orders)
    smem = pl.BlockSpec(memory_space=pltpu.SMEM)
    vmem = pl.BlockSpec(memory_space=pltpu.VMEM)
    out_count = owner_rows.shape[1]
    return pl.pallas_call(
        functools.partial(product_kernel, orders),
        out_shape=jax.ShapeDtypeStruct((out_count, block_size, width), panels.dtype),
        in_specs=[smem] * 4 + [vmem] * (1 + len(pieces)),
        out_specs=vmem,
        scratch_shapes=[
            pltpu.SMEM((step_count, keep.shape[0]), jnp.int32),
            pltpu.VMEM((step_count * block_size, width), panels.dtype),
        ],
        compiler_params=pltpu.CompilerParams(vmem_limit_bytes=48 * 1024 * 1024),
    )(place, ids, owner_rows, keep, panels, *pieces)


def flip(count, by):
    return [(i, i ^ by) for i in range(count)]


def shards(a_blocks, a_rows, b_blocks, b_occupied, keep, owner_rows):
    local_rows, _, block_size, width = b_blocks.shape
    col_blocks = keep.shape[1]
    slot_count = a_rows.shape[3]
    row_count = lax.axis_size("row")
    layer_count = lax.axis_size("layer")
    own = a_blocks.reshape(1, slot_count, block_size, block_size)
    place = jnp.stack([lax.axis_index("row"), lax.axis_index("layer")])

    def over_row(piece, by):
        return lax.ppermute(piece, "row", flip(row_count, by))

    def over_layer(piece):
        return lax.ppermute(piece, "layer", flip(layer_count, 1))

    occupied = jnp.repeat(b_occupied.reshape(local_rows, 1, 1, col_blocks), width // col_blocks, axis=3)
    masked = b_blocks * occupied.astype(b_blocks.dtype)
    panels = lax.all_gather(masked, ("col", "layer")).reshape(
        lax.axis_size("col"), layer_count, local_rows, block_size, width
    )
    held = {0: own}
    near, far = [0], row_count // 2
    while far:
        for by in near:
            held[by ^ far] = over_row(held[by], far)
        if far == row_count // 2:
            held[far], panels, a_rows = lax.optimization_barrier((held[far], panels, a_rows))
        near, far = list(held), far // 2
    ids = lax.all_gather(a_rows.reshape(slot_count), ("row", "layer")).reshape(row_count, layer_count, slot_count)
    last = row_count - 1
    held[last], ids = lax.optimization_barrier((held[last], ids))
    pieces, orders = [], []
    for by in held:
        pieces += [held[by], over_layer(held[by])]
        orders += [((by, 0),), ((by, 1),)]
    sending = product(place, ids, owner_rows[0], keep, panels, pieces, orders)
    return lax.all_to_all(sending, "col", split_axis=0, concat_axis=0, tiled=True)[None]


def solution(mesh):
    return jax.shard_map(
        shards,
        mesh=mesh,
        in_specs=(
            P(("grp", "row"), "layer", "col", None, None, None),
            P(("grp", "row"), "layer", "col", None),
            P(("grp", "col"), "layer", None, "row"),
            P(("grp", "col"), "layer", "row"),
            P(("grp", "col"), "row"),
            P(("grp", "col"), None, None),
        ),
        out_specs=P(("grp", "col", "layer"), None, None, "row"),
        check_vma=False,
    )
```

```python
import functools

import jax
import jax.numpy as jnp
from jax import lax
from jax.experimental import pallas as pl
from jax.experimental.pallas import tpu as pltpu
from jax.sharding import PartitionSpec as P

SMEM = pl.BlockSpec(memory_space=pltpu.SMEM)
VMEM = pl.BlockSpec(memory_space=pltpu.VMEM)
LIMIT = pltpu.CompilerParams(vmem_limit_bytes=48 * 1024 * 1024)
ANY = pl.BlockSpec(memory_space=pl.ANY)
TALL = 16


def turn_of(source, here, row_count):
    spots = [jnp.where(n % 2 == 1, n // 2 + 1, jnp.where(n == 0, 0, row_count - n // 2)) for n in (here, source)]
    ahead = (spots[0] - spots[1]) & (row_count - 1)
    return jnp.where(ahead == 0, 0, jnp.where(ahead <= row_count // 2, 2 * ahead - 1, 2 * (row_count - ahead)))


def prepare_kernel(a_ref, ids_ref, b_ref, occupied_ref, piece_ref, masked_ref, ids, occupied, panel, piece, done):
    rows, slot_count = a_ref.shape[0], ids.shape[1]
    local_rows, block_size, width = panel.shape
    copies = [
        pltpu.make_async_copy(ids_ref, ids, done.at[0]),
        pltpu.make_async_copy(occupied_ref, occupied, done.at[1]),
        pltpu.make_async_copy(b_ref, panel, done.at[2]),
        pltpu.make_async_copy(a_ref, piece.at[pl.ds(0, rows)], done.at[3]),
    ]
    for copy in copies:
        copy.start()
    copies[0].wait()
    line = lax.broadcasted_iota(jnp.int32, (TALL, block_size), 0)
    listed = jnp.full(line.shape, -1, jnp.int32)
    for s in range(slot_count):
        listed = jnp.where(line == s, ids[0, s], listed)
    piece[rows:, :] = listed.astype(jnp.float32).astype(piece.dtype)
    copies[3].wait()
    piece_out = pltpu.make_async_copy(piece, piece_ref, done.at[4])
    piece_out.start()
    copies[1].wait()
    copies[2].wait()
    lane = lax.broadcasted_iota(jnp.int32, (1, width), 1)
    for j in range(local_rows):
        kept = jnp.zeros((1, width), jnp.int32)
        for n in range(width // block_size):
            kept = jnp.where(lane // block_size == n, occupied[j, n], kept)
        panel[j] = panel[j] * kept.astype(jnp.float32).astype(panel.dtype)
    panel_out = pltpu.make_async_copy(panel, masked_ref, done.at[5])
    panel_out.start()
    piece_out.wait()
    panel_out.wait()


def prepare(blocks, ids, b_blocks, occupied):
    rows, block_size = blocks.shape
    return pl.pallas_call(
        prepare_kernel,
        out_shape=(
            jax.ShapeDtypeStruct((rows + TALL, block_size), blocks.dtype),
            jax.ShapeDtypeStruct(b_blocks.shape, b_blocks.dtype),
        ),
        in_specs=[ANY] * 4,
        out_specs=(ANY, ANY),
        scratch_shapes=[
            pltpu.SMEM(ids.shape, jnp.int32),
            pltpu.SMEM(occupied.shape, jnp.int32),
            pltpu.VMEM(b_blocks.shape, b_blocks.dtype),
            pltpu.VMEM((rows + TALL, block_size), blocks.dtype),
            pltpu.SemaphoreType.DMA((6,)),
        ],
        compiler_params=pltpu.CompilerParams(vmem_limit_bytes=60 * 1024 * 1024),
    )(blocks, ids, b_blocks, occupied)


def early_kernel(slot_count, owner_ref, keep_ref, *refs):
    layer_count, half_rows = owner_ref.shape
    col_count = half_rows // layer_count
    slab_ref, twin_ref, *piece_refs, total_ref, last_ref, chosen_ref, kept_ref, listed, ids, slots, panels, done = refs
    steps = len(piece_refs)
    block_size = piece_refs[0].shape[1]
    rows = slot_count * block_size
    _, local_rows, _, width = slab_ref.shape
    row, col, layer = (lax.axis_index(name) for name in ("row", "col", "layer"))
    for n, ref in enumerate(piece_refs):
        listed[n] = ref[rows : rows + TALL, :].astype(jnp.float32).astype(jnp.int32)
    copy = pltpu.make_async_copy(listed, ids, done)
    copy.start()
    for n in range(steps):
        for m in range(slots.shape[1]):
            slots[n, m] = -1
    for flip_col in range(col_count):
        for flip_layer, ref in enumerate((slab_ref, twin_ref)):
            for j in range(local_rows):
                turn = turn_of((col ^ flip_col) * local_rows + j, row, col_count * local_rows)
                panels[turn * layer_count + flip_layer] = ref[flip_col, j]
    for n in range(layer_count):
        last_ref[n * block_size : (n + 1) * block_size, :] = panels[steps + n]
    copy.wait()
    for n in range(steps):
        for s in range(slot_count):
            slots[n, ids[n, s, 0]] = s
    lane = lax.broadcasted_iota(jnp.int32, (1, width), 1)
    lines = []
    for q in range(total_ref.shape[0]):
        half = q % layer_count
        m = half * half_rows + owner_ref[half, (col ^ (q // layer_count)) * layer_count + layer]
        parts = []
        for n, ref in enumerate(piece_refs):
            s = slots[n, m]
            block = ref[pl.ds(pl.multiple_of(jnp.maximum(s, 0) * block_size, block_size), block_size), :]
            parts.append(jnp.where(s >= 0, block, jnp.zeros_like(block)))
        lines.append(jnp.concatenate(parts, axis=1))
        kept = jnp.zeros((1, width), jnp.int32)
        for n in range(width // block_size):
            kept = jnp.where(lane // block_size == n, keep_ref[n, m], kept)
        kept_ref[q : q + 1, :] = kept.astype(jnp.float32)
        chosen_ref[q : q + 1, :] = jnp.full((1, block_size), m, jnp.int32).astype(jnp.float32)
        if half == layer_count - 1:
            total = jnp.dot(
                jnp.concatenate(lines, axis=0),
                panels[:steps].reshape(steps * block_size, width),
                preferred_element_type=jnp.float32,
            )
            for n in range(layer_count):
                total_ref[q - half + n] = total[n * block_size : (n + 1) * block_size]
            lines = []


def early(slot_count, owner_rows, keep, slabs, twins, pieces):
    layer_count, out_count = owner_rows.shape
    block_size, width = slabs.shape[2:]
    steps, kind = len(pieces), slabs.dtype
    return pl.pallas_call(
        functools.partial(early_kernel, slot_count),
        out_shape=(
            jax.ShapeDtypeStruct((out_count, block_size, width), jnp.float32),
            jax.ShapeDtypeStruct((layer_count * block_size, width), kind),
            jax.ShapeDtypeStruct((out_count, block_size), jnp.float32),
            jax.ShapeDtypeStruct((out_count, width), jnp.float32),
        ),
        in_specs=[SMEM] * 2 + [VMEM] * (2 + steps),
        out_specs=[VMEM] * 4,
        scratch_shapes=[
            pltpu.VMEM((steps, TALL, block_size), jnp.int32),
            pltpu.SMEM((steps, TALL, block_size), jnp.int32),
            pltpu.SMEM((steps, keep.shape[1]), jnp.int32),
            pltpu.VMEM((steps + layer_count, block_size, width), kind),
            pltpu.SemaphoreType.DMA,
        ],
        compiler_params=LIMIT,
    )(owner_rows, keep, slabs, twins, *pieces)


def late_kernel(slot_count, total_ref, last_ref, chosen_ref, kept_ref, *refs):
    layer_count = last_ref.shape[0] // total_ref.shape[1]
    piece_refs, out_refs = refs[:layer_count], refs[layer_count:]
    block_size = total_ref.shape[1]
    rows = slot_count * block_size
    listed = [ref[rows : rows + TALL, :].astype(jnp.float32) for ref in piece_refs]
    for at, out_ref in enumerate(out_refs):
        lines = []
        for q in range(at * layer_count, (at + 1) * layer_count):
            parts = []
            for n, ref in enumerate(piece_refs):
                part = None
                for s in range(slot_count):
                    same = (listed[n][s : s + 1, :] == chosen_ref[q : q + 1, :]).astype(jnp.float32)
                    same = jnp.broadcast_to(same, (TALL, block_size)).astype(ref.dtype)
                    same = jnp.concatenate([same] * (block_size // TALL), axis=0)
                    block = ref[s * block_size : (s + 1) * block_size, :] * same
                    part = block if part is None else part + block
                parts.append(part)
            lines.append(jnp.concatenate(parts, axis=1))
        total = jnp.dot(jnp.concatenate(lines, axis=0), last_ref[...], preferred_element_type=jnp.float32)
        for n in range(layer_count):
            q = at * layer_count + n
            part = total[n * block_size : (n + 1) * block_size] + total_ref[q]
            out_ref[n] = (part * kept_ref[q : q + 1, :]).astype(out_ref.dtype)


def late(slot_count, totals, pieces):
    total, last = totals[:2]
    out_count, block_size, width = total.shape
    layer_count = last.shape[0] // block_size
    shape = jax.ShapeDtypeStruct((layer_count, block_size, width), last.dtype)
    return pl.pallas_call(
        functools.partial(late_kernel, slot_count),
        out_shape=[shape] * (out_count // layer_count),
        in_specs=[VMEM] * (4 + layer_count),
        out_specs=[VMEM] * (out_count // layer_count),
        compiler_params=LIMIT,
    )(*totals, *pieces)


def collect_kernel(*refs):
    *part_refs, out_ref, done = refs
    count, col = part_refs[0].shape[0], lax.axis_index("col")
    copies = []
    for flip_col, ref in enumerate(part_refs):
        at = pl.multiple_of((col ^ flip_col) * count, count)
        copies.append(pltpu.make_async_copy(ref, out_ref.at[pl.ds(at, count)], done.at[flip_col]))
    for copy in copies:
        copy.start()
    for copy in copies:
        copy.wait()


def collect(parts):
    count, block_size, width = parts[0].shape
    return pl.pallas_call(
        collect_kernel,
        out_shape=jax.ShapeDtypeStruct((count * len(parts), block_size, width), parts[0].dtype),
        in_specs=[VMEM] * len(parts),
        out_specs=ANY,
        scratch_shapes=[pltpu.SemaphoreType.DMA((len(parts),))],
        compiler_params=LIMIT,
    )(*parts)


def swap(value, axis, by):
    return lax.ppermute(value, axis, [(i, i ^ by) for i in range(lax.axis_size(axis))])


def shards(a_blocks, a_rows, b_blocks, b_occupied, keep, owner_rows):
    local_rows, _, block_size, width = b_blocks.shape
    slot_count = a_rows.shape[3]
    row_count, col_count, layer_count = (lax.axis_size(name) for name in ("row", "col", "layer"))
    ring = list(range(0, row_count, 2))[:1] + list(range(1, row_count, 2)) + list(range(row_count - 2, 0, -2))
    turns = [(n // 2 + 1) * (1 if n % 2 == 0 else -1) for n in range(row_count - 1)]
    turns = [0] + sorted(turns, key=abs)

    own, masked = prepare(
        a_blocks.reshape(slot_count * block_size, block_size),
        a_rows.reshape(1, slot_count),
        b_blocks.reshape(local_rows, block_size, width),
        b_occupied.reshape(local_rows, -1),
    )
    held, slabs = {0: own}, [masked]
    for turn in turns[1:]:
        step = 1 if turn > 0 else -1
        before = held[turn - step]
        held[turn] = lax.ppermute(
            before, "row", [(name, ring[(at + step) % row_count]) for at, name in enumerate(ring)]
        )
        if turn == turns[2]:
            slabs += [swap(masked, "col", by) for by in range(1, col_count)]
    slabs = jnp.stack(slabs)
    twins = swap(slabs, "layer", 1)
    pieces = []
    for turn in turns[:-1]:
        pieces += [held[turn], swap(held[turn], "layer", 1)]
    totals = early(slot_count, owner_rows[0], keep.T, slabs, twins, pieces)
    final = held[turns[-1]]
    parts = list(late(slot_count, totals, [final, swap(final, "layer", 1)]))
    for by in sorted(range(1, col_count), key=lambda n: -bin(n).count("1")):
        parts[by] = swap(parts[by], "col", by)
    return collect(parts)[None]


def solution(mesh):
    return jax.shard_map(
        shards,
        mesh=mesh,
        in_specs=(
            P(("grp", "row"), "layer", "col", None, None, None),
            P(("grp", "row"), "layer", "col", None),
            P(("grp", "col"), "layer", None, "row"),
            P(("grp", "col"), "layer", "row"),
            P(("grp", "col"), "row"),
            P(("grp", "col"), None, None),
        ),
        out_specs=P(("grp", "col", "layer"), None, None, "row"),
        check_vma=False,
    )
```

```python
import functools

import jax
import jax.numpy as jnp
from jax import lax
from jax.experimental import pallas as pl
from jax.experimental.pallas import tpu as pltpu
from jax.sharding import PartitionSpec as P

SMEM = pl.BlockSpec(memory_space=pltpu.SMEM)
VMEM = pl.BlockSpec(memory_space=pltpu.VMEM)
LIMIT = pltpu.CompilerParams(vmem_limit_bytes=48 * 1024 * 1024)
ANY = pl.BlockSpec(memory_space=pl.ANY)
TALL = 16


def turn_of(source, here, row_count):
    spots = [jnp.where(n % 2 == 1, n // 2 + 1, jnp.where(n == 0, 0, row_count - n // 2)) for n in (here, source)]
    ahead = (spots[0] - spots[1]) & (row_count - 1)
    return jnp.where(ahead == 0, 0, jnp.where(ahead <= row_count // 2, 2 * ahead - 1, 2 * (row_count - ahead)))


def prepare_kernel(a_ref, ids_ref, b_ref, occupied_ref, piece_ref, masked_ref, ids, occupied, panel, piece, done):
    rows, slot_count = a_ref.shape[0], ids.shape[1]
    local_rows, block_size, width = panel.shape
    copies = [
        pltpu.make_async_copy(ids_ref, ids, done.at[0]),
        pltpu.make_async_copy(occupied_ref, occupied, done.at[1]),
        pltpu.make_async_copy(b_ref, panel, done.at[2]),
        pltpu.make_async_copy(a_ref, piece.at[pl.ds(0, rows)], done.at[3]),
    ]
    for copy in copies:
        copy.start()
    copies[0].wait()
    line = lax.broadcasted_iota(jnp.int32, (TALL, block_size), 0)
    listed = jnp.full(line.shape, -1, jnp.int32)
    for s in range(slot_count):
        listed = jnp.where(line == s, ids[0, s], listed)
    piece[rows:, :] = listed.astype(jnp.float32).astype(piece.dtype)
    copies[3].wait()
    piece_out = pltpu.make_async_copy(piece, piece_ref, done.at[4])
    piece_out.start()
    copies[1].wait()
    copies[2].wait()
    lane = lax.broadcasted_iota(jnp.int32, (1, width), 1)
    for j in range(local_rows):
        kept = jnp.zeros((1, width), jnp.int32)
        for n in range(width // block_size):
            kept = jnp.where(lane // block_size == n, occupied[j, n], kept)
        panel[j] = panel[j] * kept.astype(jnp.float32).astype(panel.dtype)
    panel_out = pltpu.make_async_copy(panel, masked_ref, done.at[5])
    panel_out.start()
    piece_out.wait()
    panel_out.wait()


def prepare(blocks, ids, b_blocks, occupied):
    rows, block_size = blocks.shape
    return pl.pallas_call(
        prepare_kernel,
        out_shape=(
            jax.ShapeDtypeStruct((rows + TALL, block_size), blocks.dtype),
            jax.ShapeDtypeStruct(b_blocks.shape, b_blocks.dtype),
        ),
        in_specs=[ANY] * 4,
        out_specs=(ANY, ANY),
        scratch_shapes=[
            pltpu.SMEM(ids.shape, jnp.int32),
            pltpu.SMEM(occupied.shape, jnp.int32),
            pltpu.VMEM(b_blocks.shape, b_blocks.dtype),
            pltpu.VMEM((rows + TALL, block_size), blocks.dtype),
            pltpu.SemaphoreType.DMA((6,)),
        ],
        compiler_params=pltpu.CompilerParams(vmem_limit_bytes=60 * 1024 * 1024),
    )(blocks, ids, b_blocks, occupied)


def choose_kernel(owner_ref, keep_ref, chosen_ref, kept_ref):
    layer_count, half_rows = owner_ref.shape
    out_count, block_size = chosen_ref.shape
    width = kept_ref.shape[1]
    col, layer = lax.axis_index("col"), lax.axis_index("layer")
    lane = lax.broadcasted_iota(jnp.int32, (1, width), 1)
    for q in range(out_count):
        half = q % layer_count
        m = half * half_rows + owner_ref[half, (col ^ (q // layer_count)) * layer_count + layer]
        kept = jnp.zeros((1, width), jnp.int32)
        for n in range(width // block_size):
            kept = jnp.where(lane // block_size == n, keep_ref[n, m], kept)
        kept_ref[q : q + 1, :] = kept.astype(jnp.float32)
        chosen_ref[q : q + 1, :] = jnp.full((1, block_size), m, jnp.int32).astype(jnp.float32)


def choose(owner_rows, keep, block_size):
    out_count = owner_rows.shape[1]
    return pl.pallas_call(
        choose_kernel,
        out_shape=(
            jax.ShapeDtypeStruct((out_count, block_size), jnp.float32),
            jax.ShapeDtypeStruct((out_count, keep.shape[0] * block_size), jnp.float32),
        ),
        in_specs=[SMEM] * 2,
        out_specs=[VMEM] * 2,
        compiler_params=LIMIT,
    )(owner_rows, keep)


def pick(slot_count, piece_refs, chosen_ref, queries):
    block_size = chosen_ref.shape[1]
    rows = slot_count * block_size
    listed = [ref[rows : rows + TALL, :].astype(jnp.float32) for ref in piece_refs]
    lines = []
    for q in queries:
        parts = []
        for n, ref in enumerate(piece_refs):
            part = None
            for s in range(slot_count):
                same = (listed[n][s : s + 1, :] == chosen_ref[pl.ds(q, 1), :]).astype(jnp.float32)
                same = jnp.broadcast_to(same, (TALL, block_size)).astype(ref.dtype)
                same = jnp.concatenate([same] * (block_size // TALL), axis=0)
                block = ref[s * block_size : (s + 1) * block_size, :] * same
                part = block if part is None else part + block
            parts.append(part)
        lines.append(jnp.concatenate(parts, axis=1))
    return jnp.concatenate(lines, axis=0)


def early_kernel(slot_count, chosen_ref, slab_ref, twin_ref, *refs):
    *piece_refs, total_ref, last_ref, panels = refs
    steps = len(piece_refs)
    col_count, local_rows, block_size, width = slab_ref.shape
    out_count = total_ref.shape[0]
    layer_count = out_count // col_count
    row, col = lax.axis_index("row"), lax.axis_index("col")
    for flip_col in range(col_count):
        for flip_layer, ref in enumerate((slab_ref, twin_ref)):
            for j in range(local_rows):
                turn = turn_of((col ^ flip_col) * local_rows + j, row, col_count * local_rows)
                panels[turn * layer_count + flip_layer] = ref[flip_col, j]
    for n in range(last_ref.shape[0] // block_size):
        last_ref[n * block_size : (n + 1) * block_size, :] = panels[steps + n]

    def add(at, carry):
        queries = [at * layer_count + n for n in range(layer_count)]
        total = jnp.dot(
            pick(slot_count, piece_refs, chosen_ref, queries),
            panels[:steps].reshape(steps * block_size, width),
            preferred_element_type=jnp.float32,
        )
        for n, q in enumerate(queries):
            total_ref[q] = total[n * block_size : (n + 1) * block_size]
        return carry

    if steps > 16:
        lax.fori_loop(0, col_count, add, 0)
    else:
        for at in range(col_count):
            add(at, 0)


def early(slot_count, late_count, chosen, slabs, twins, pieces):
    block_size, width = slabs.shape[2:]
    steps, kind = len(pieces), slabs.dtype
    return pl.pallas_call(
        functools.partial(early_kernel, slot_count),
        out_shape=(
            jax.ShapeDtypeStruct((chosen.shape[0], block_size, width), jnp.float32),
            jax.ShapeDtypeStruct((late_count * block_size, width), kind),
        ),
        in_specs=[VMEM] * (3 + steps),
        out_specs=[VMEM] * 2,
        scratch_shapes=[pltpu.VMEM((steps + late_count, block_size, width), kind)],
        compiler_params=LIMIT,
    )(chosen, slabs, twins, *pieces)


def late_kernel(slot_count, col_count, total_ref, last_ref, chosen_ref, kept_ref, *refs):
    piece_refs, out_refs = refs[:-col_count], refs[-col_count:]
    block_size = total_ref.shape[1]
    layer_count = total_ref.shape[0] // col_count
    for at, out_ref in enumerate(out_refs):
        queries = range(at * layer_count, (at + 1) * layer_count)
        lines = pick(slot_count, piece_refs, chosen_ref, queries)
        total = jnp.dot(lines, last_ref[...], preferred_element_type=jnp.float32)
        for n, q in enumerate(queries):
            part = total[n * block_size : (n + 1) * block_size] + total_ref[q]
            out_ref[n] = (part * kept_ref[q : q + 1, :]).astype(out_ref.dtype)


def late(slot_count, col_count, totals, chosen, kept, pieces):
    total, last = totals
    out_count, block_size, width = total.shape
    shape = jax.ShapeDtypeStruct((out_count // col_count, block_size, width), last.dtype)
    return pl.pallas_call(
        functools.partial(late_kernel, slot_count, col_count),
        out_shape=[shape] * col_count,
        in_specs=[VMEM] * (4 + len(pieces)),
        out_specs=[VMEM] * col_count,
        compiler_params=LIMIT,
    )(total, last, chosen, kept, *pieces)


def collect_kernel(*refs):
    *part_refs, out_ref, done = refs
    count, col = part_refs[0].shape[0], lax.axis_index("col")
    copies = []
    for flip_col, ref in enumerate(part_refs[::-1]):
        at = pl.multiple_of((col ^ flip_col) * count, count)
        copies.append(pltpu.make_async_copy(ref, out_ref.at[pl.ds(at, count)], done.at[flip_col]))
    for copy in copies:
        copy.start()
    for copy in copies:
        copy.wait()


def collect(parts):
    count, block_size, width = parts[0].shape
    return pl.pallas_call(
        collect_kernel,
        out_shape=jax.ShapeDtypeStruct((count * len(parts), block_size, width), parts[0].dtype),
        in_specs=[VMEM] * len(parts),
        out_specs=ANY,
        scratch_shapes=[pltpu.SemaphoreType.DMA((len(parts),))],
        compiler_params=LIMIT,
    )(*parts[::-1])


def swap(value, axis, by):
    return lax.ppermute(value, axis, [(i, i ^ by) for i in range(lax.axis_size(axis))])


def shards(a_blocks, a_rows, b_blocks, b_occupied, keep, owner_rows):
    local_rows, _, block_size, width = b_blocks.shape
    slot_count = a_rows.shape[3]
    row_count, col_count, layer_count = (lax.axis_size(name) for name in ("row", "col", "layer"))
    ring = list(range(0, row_count, 2))[:1] + list(range(1, row_count, 2)) + list(range(row_count - 2, 0, -2))
    turns = [(n // 2 + 1) * (1 if n % 2 == 0 else -1) for n in range(row_count - 1)]
    turns = [0] + sorted(turns, key=abs)

    own, masked = prepare(
        a_blocks.reshape(slot_count * block_size, block_size),
        a_rows.reshape(1, slot_count),
        b_blocks.reshape(local_rows, block_size, width),
        b_occupied.reshape(local_rows, -1),
    )
    chosen, kept = choose(owner_rows[0], keep.T, block_size)
    slabs = [masked] + [swap(masked, "col", by) for by in range(1, col_count)]
    chosen, kept, *slabs = lax.optimization_barrier((chosen, kept, *slabs))
    slabs = jnp.stack(slabs)
    twins = swap(slabs, "layer", 1)
    held = {0: own}
    for turn in turns[1:]:
        step = 1 if turn > 0 else -1
        held[turn] = lax.ppermute(
            held[turn - step], "row", [(name, ring[(at + step) % row_count]) for at, name in enumerate(ring)]
        )
    split = row_count - 1
    pieces = [one for turn in turns for one in (held[turn], swap(held[turn], "layer", 1))]
    steps = split * layer_count
    totals = early(slot_count, len(pieces) - steps, chosen, slabs, twins, pieces[:steps])
    parts = list(late(slot_count, col_count, totals, chosen, kept, pieces[steps:]))
    for by in sorted(range(1, col_count), key=lambda n: -bin(n).count("1")):
        parts[by] = swap(parts[by], "col", by)
    return collect(parts)[None]


def solution(mesh):
    return jax.shard_map(
        shards,
        mesh=mesh,
        in_specs=(
            P(("grp", "row"), "layer", "col", None, None, None),
            P(("grp", "row"), "layer", "col", None),
            P(("grp", "col"), "layer", None, "row"),
            P(("grp", "col"), "layer", "row"),
            P(("grp", "col"), "row"),
            P(("grp", "col"), None, None),
        ),
        out_specs=P(("grp", "col", "layer"), None, None, "row"),
        check_vma=False,
    )
```

```python
import functools

import jax
import jax.numpy as jnp
from jax import lax
from jax.experimental import pallas as pl
from jax.experimental.pallas import tpu as pltpu
from jax.sharding import PartitionSpec as P

SMEM = pl.BlockSpec(memory_space=pltpu.SMEM)
VMEM = pl.BlockSpec(memory_space=pltpu.VMEM)
LIMIT = pltpu.CompilerParams(vmem_limit_bytes=48 * 1024 * 1024)
ANY = pl.BlockSpec(memory_space=pl.ANY)
TALL = 16


def turn_of(source, here, row_count):
    spots = [jnp.where(n % 2 == 1, n // 2 + 1, jnp.where(n == 0, 0, row_count - n // 2)) for n in (here, source)]
    ahead = (spots[1] - spots[0]) & (row_count - 1)
    return jnp.where(ahead == 0, 0, jnp.where(ahead <= row_count // 2, 2 * ahead - 1, 2 * (row_count - ahead)))


def prepare_kernel(a_ref, ids_ref, b_ref, occupied_ref, piece_ref, masked_ref, ids, occupied, panel, piece, done):
    rows, slot_count = a_ref.shape[0], ids.shape[1]
    local_rows, block_size, width = panel.shape
    copies = [
        pltpu.make_async_copy(ids_ref, ids, done.at[0]),
        pltpu.make_async_copy(occupied_ref, occupied, done.at[1]),
        pltpu.make_async_copy(b_ref, panel, done.at[2]),
        pltpu.make_async_copy(a_ref, piece.at[pl.ds(0, rows)], done.at[3]),
    ]
    for copy in copies:
        copy.start()
    copies[0].wait()
    line = lax.broadcasted_iota(jnp.int32, (TALL, block_size), 0)
    listed = jnp.full(line.shape, -1, jnp.int32)
    for s in range(slot_count):
        listed = jnp.where(line == s, ids[0, s], listed)
    piece[rows:, :] = listed.astype(jnp.float32).astype(piece.dtype)
    copies[3].wait()
    piece_out = pltpu.make_async_copy(piece, piece_ref, done.at[4])
    piece_out.start()
    copies[1].wait()
    copies[2].wait()
    lane = lax.broadcasted_iota(jnp.int32, (1, width), 1)
    for j in range(local_rows):
        kept = jnp.zeros((1, width), jnp.int32)
        for n in range(width // block_size):
            kept = jnp.where(lane // block_size == n, occupied[j, n], kept)
        panel[j] = panel[j] * kept.astype(jnp.float32).astype(panel.dtype)
    panel_out = pltpu.make_async_copy(panel, masked_ref, done.at[5])
    panel_out.start()
    piece_out.wait()
    panel_out.wait()


def prepare(blocks, ids, b_blocks, occupied):
    rows, block_size = blocks.shape
    return pl.pallas_call(
        prepare_kernel,
        out_shape=(
            jax.ShapeDtypeStruct((rows + TALL, block_size), blocks.dtype),
            jax.ShapeDtypeStruct(b_blocks.shape, b_blocks.dtype),
        ),
        in_specs=[ANY] * 4,
        out_specs=(ANY, ANY),
        scratch_shapes=[
            pltpu.SMEM(ids.shape, jnp.int32),
            pltpu.SMEM(occupied.shape, jnp.int32),
            pltpu.VMEM(b_blocks.shape, b_blocks.dtype),
            pltpu.VMEM((rows + TALL, block_size), blocks.dtype),
            pltpu.SemaphoreType.DMA((6,)),
        ],
        compiler_params=pltpu.CompilerParams(vmem_limit_bytes=60 * 1024 * 1024),
    )(blocks, ids, b_blocks, occupied)


def choose_kernel(owner_ref, keep_ref, chosen_ref, kept_ref):
    layer_count, half_rows = owner_ref.shape
    out_count, block_size = chosen_ref.shape
    width = kept_ref.shape[1]
    col, layer = lax.axis_index("col"), lax.axis_index("layer")
    lane = lax.broadcasted_iota(jnp.int32, (1, width), 1)
    for q in range(out_count):
        half = q % layer_count
        m = half * half_rows + owner_ref[half, (col ^ (q // layer_count)) * layer_count + layer]
        kept = jnp.zeros((1, width), jnp.int32)
        for n in range(width // block_size):
            kept = jnp.where(lane // block_size == n, keep_ref[n, m], kept)
        kept_ref[q : q + 1, :] = kept.astype(jnp.float32)
        chosen_ref[q : q + 1, :] = jnp.full((1, block_size), m, jnp.int32).astype(jnp.float32)


def choose(owner_rows, keep, block_size):
    out_count = owner_rows.shape[1]
    return pl.pallas_call(
        choose_kernel,
        out_shape=(
            jax.ShapeDtypeStruct((out_count, block_size), jnp.float32),
            jax.ShapeDtypeStruct((out_count, keep.shape[0] * block_size), jnp.float32),
        ),
        in_specs=[SMEM] * 2,
        out_specs=[VMEM] * 2,
        compiler_params=LIMIT,
    )(owner_rows, keep)


def pick(slot_count, piece_refs, chosen_ref, queries):
    block_size = chosen_ref.shape[1]
    rows = slot_count * block_size
    listed = [ref[rows : rows + TALL, :].astype(jnp.float32) for ref in piece_refs]
    lines = []
    for q in queries:
        parts = []
        for n, ref in enumerate(piece_refs):
            part = None
            for s in range(slot_count):
                same = (listed[n][s : s + 1, :] == chosen_ref[pl.ds(q, 1), :]).astype(jnp.float32)
                same = jnp.broadcast_to(same, (TALL, block_size)).astype(ref.dtype)
                same = jnp.concatenate([same] * (block_size // TALL), axis=0)
                block = ref[s * block_size : (s + 1) * block_size, :] * same
                part = block if part is None else part + block
            parts.append(part)
        lines.append(jnp.concatenate(parts, axis=1))
    return jnp.concatenate(lines, axis=0)


def early_kernel(slot_count, chosen_ref, slab_ref, twin_ref, *refs):
    *piece_refs, total_ref, last_ref, panels = refs
    steps = len(piece_refs)
    col_count, local_rows, block_size, width = slab_ref.shape
    out_count = total_ref.shape[0]
    layer_count = out_count // col_count
    row, col = lax.axis_index("row"), lax.axis_index("col")
    for flip_col in range(col_count):
        for flip_layer, ref in enumerate((slab_ref, twin_ref)):
            for j in range(local_rows):
                turn = turn_of((col ^ flip_col) * local_rows + j, row, col_count * local_rows)
                panels[turn * layer_count + flip_layer] = ref[flip_col, j]
    for n in range(last_ref.shape[0] // block_size):
        last_ref[n * block_size : (n + 1) * block_size, :] = panels[steps + n]

    def add(at, carry):
        queries = [at * layer_count + n for n in range(layer_count)]
        total = jnp.dot(
            pick(slot_count, piece_refs, chosen_ref, queries),
            panels[:steps].reshape(steps * block_size, width),
            preferred_element_type=jnp.float32,
        )
        for n, q in enumerate(queries):
            total_ref[q] = total[n * block_size : (n + 1) * block_size]
        return carry

    if steps > 16:
        lax.fori_loop(0, col_count, add, 0)
    else:
        for at in range(col_count):
            add(at, 0)


def early(slot_count, late_count, chosen, slabs, twins, pieces):
    block_size, width = slabs.shape[2:]
    steps, kind = len(pieces), slabs.dtype
    return pl.pallas_call(
        functools.partial(early_kernel, slot_count),
        out_shape=(
            jax.ShapeDtypeStruct((chosen.shape[0], block_size, width), jnp.float32),
            jax.ShapeDtypeStruct((late_count * block_size, width), kind),
        ),
        in_specs=[VMEM] * (3 + steps),
        out_specs=[VMEM] * 2,
        scratch_shapes=[pltpu.VMEM((steps + late_count, block_size, width), kind)],
        compiler_params=LIMIT,
    )(chosen, slabs, twins, *pieces)


def late_kernel(slot_count, col_count, total_ref, last_ref, chosen_ref, kept_ref, *refs):
    piece_refs, out_refs = refs[:-col_count], refs[-col_count:]
    block_size = total_ref.shape[1]
    layer_count = total_ref.shape[0] // col_count
    for at, out_ref in enumerate(out_refs):
        queries = range(at * layer_count, (at + 1) * layer_count)
        lines = pick(slot_count, piece_refs, chosen_ref, queries)
        total = jnp.dot(lines, last_ref[...], preferred_element_type=jnp.float32)
        for n, q in enumerate(queries):
            part = total[n * block_size : (n + 1) * block_size] + total_ref[q]
            out_ref[n] = (part * kept_ref[q : q + 1, :]).astype(out_ref.dtype)


def late(slot_count, col_count, totals, chosen, kept, pieces):
    total, last = totals
    out_count, block_size, width = total.shape
    shape = jax.ShapeDtypeStruct((out_count // col_count, block_size, width), last.dtype)
    return pl.pallas_call(
        functools.partial(late_kernel, slot_count, col_count),
        out_shape=[shape] * col_count,
        in_specs=[VMEM] * (4 + len(pieces)),
        out_specs=[VMEM] * col_count,
        compiler_params=LIMIT,
    )(total, last, chosen, kept, *pieces)


def collect_kernel(*refs):
    *part_refs, out_ref, done = refs
    count, col = part_refs[0].shape[0], lax.axis_index("col")
    copies = []
    for flip_col, ref in enumerate(part_refs[::-1]):
        at = pl.multiple_of((col ^ flip_col) * count, count)
        copies.append(pltpu.make_async_copy(ref, out_ref.at[pl.ds(at, count)], done.at[flip_col]))
    for copy in copies:
        copy.start()
    for copy in copies:
        copy.wait()


def collect(parts):
    count, block_size, width = parts[0].shape
    return pl.pallas_call(
        collect_kernel,
        out_shape=jax.ShapeDtypeStruct((count * len(parts), block_size, width), parts[0].dtype),
        in_specs=[VMEM] * len(parts),
        out_specs=ANY,
        scratch_shapes=[pltpu.SemaphoreType.DMA((len(parts),))],
        compiler_params=LIMIT,
    )(*parts[::-1])


def swap(value, axis, by):
    return lax.ppermute(value, axis, [(i, i ^ by) for i in range(lax.axis_size(axis))])


def shards(a_blocks, a_rows, b_blocks, b_occupied, keep, owner_rows):
    local_rows, _, block_size, width = b_blocks.shape
    slot_count = a_rows.shape[3]
    row_count, col_count, layer_count = (lax.axis_size(name) for name in ("row", "col", "layer"))
    ring = list(range(0, row_count, 2)) + list(range(row_count - 1, 0, -2))
    turns = [(n // 2 + 1) * (1 if n % 2 == 0 else -1) for n in range(row_count - 1)]
    turns = [0] + sorted(turns, key=abs)

    own, masked = prepare(
        a_blocks.reshape(slot_count * block_size, block_size),
        a_rows.reshape(1, slot_count),
        b_blocks.reshape(local_rows, block_size, width),
        b_occupied.reshape(local_rows, -1),
    )
    chosen, kept = choose(owner_rows[0], keep.T, block_size)
    slabs = [masked] + [swap(masked, "col", by) for by in range(1, col_count)]
    chosen, kept, *slabs = lax.optimization_barrier((chosen, kept, *slabs))
    slabs = jnp.stack(slabs)
    twins = swap(slabs, "layer", 1)
    held = {0: own}
    for turn in turns[1:]:
        step = 1 if turn > 0 else -1
        held[turn] = lax.ppermute(
            held[turn - step], "row", [(name, ring[(at + step) % row_count]) for at, name in enumerate(ring)]
        )
    split = row_count - 1
    pieces = [one for turn in turns for one in (held[turn], swap(held[turn], "layer", 1))]
    steps = split * layer_count
    totals = early(slot_count, len(pieces) - steps, chosen, slabs, twins, pieces[:steps])
    parts = list(late(slot_count, col_count, totals, chosen, kept, pieces[steps:]))
    for by in sorted(range(1, col_count), key=lambda n: -bin(n).count("1")):
        parts[by] = swap(parts[by], "col", by)
    return collect(parts)[None]


def solution(mesh):
    return jax.shard_map(
        shards,
        mesh=mesh,
        in_specs=(
            P(("grp", "row"), "layer", "col", None, None, None),
            P(("grp", "row"), "layer", "col", None),
            P(("grp", "col"), "layer", None, "row"),
            P(("grp", "col"), "layer", "row"),
            P(("grp", "col"), "row"),
            P(("grp", "col"), None, None),
        ),
        out_specs=P(("grp", "col", "layer"), None, None, "row"),
        check_vma=False,
    )
```

```python
import functools

import jax
import jax.numpy as jnp
from jax import lax
from jax.experimental import pallas as pl
from jax.experimental.pallas import tpu as pltpu
from jax.sharding import PartitionSpec as P

SMEM = pl.BlockSpec(memory_space=pltpu.SMEM)
VMEM = pl.BlockSpec(memory_space=pltpu.VMEM)
LIMIT = pltpu.CompilerParams(vmem_limit_bytes=48 * 1024 * 1024)
ANY = pl.BlockSpec(memory_space=pl.ANY)
TALL = 16


def turn_of(source, here, row_count):
    spots = [jnp.where(n % 2 == 1, n // 2 + 1, jnp.where(n == 0, 0, row_count - n // 2)) for n in (here, source)]
    ahead = (spots[1] - spots[0]) & (row_count - 1)
    return jnp.where(ahead == 0, 0, jnp.where(ahead <= row_count // 2, 2 * ahead - 1, 2 * (row_count - ahead)))


def prepare_kernel(a_ref, ids_ref, b_ref, occupied_ref, piece_ref, masked_ref, ids, occupied, panel, piece, done):
    rows, slot_count = a_ref.shape[0], ids.shape[1]
    local_rows, block_size, width = panel.shape
    copies = [
        pltpu.make_async_copy(ids_ref, ids, done.at[0]),
        pltpu.make_async_copy(occupied_ref, occupied, done.at[1]),
        pltpu.make_async_copy(b_ref, panel, done.at[2]),
        pltpu.make_async_copy(a_ref, piece.at[pl.ds(0, rows)], done.at[3]),
    ]
    for copy in copies:
        copy.start()
    copies[0].wait()
    line = lax.broadcasted_iota(jnp.int32, (TALL, block_size), 0)
    listed = jnp.full(line.shape, -1, jnp.int32)
    for s in range(slot_count):
        listed = jnp.where(line == s, ids[0, s], listed)
    piece[rows:, :] = listed.astype(jnp.float32).astype(piece.dtype)
    copies[3].wait()
    piece_out = pltpu.make_async_copy(piece, piece_ref, done.at[4])
    piece_out.start()
    copies[1].wait()
    copies[2].wait()
    lane = lax.broadcasted_iota(jnp.int32, (1, width), 1)
    for j in range(local_rows):
        kept = jnp.zeros((1, width), jnp.int32)
        for n in range(width // block_size):
            kept = jnp.where(lane // block_size == n, occupied[j, n], kept)
        panel[j] = panel[j] * kept.astype(jnp.float32).astype(panel.dtype)
    panel_out = pltpu.make_async_copy(panel, masked_ref, done.at[5])
    panel_out.start()
    piece_out.wait()
    panel_out.wait()


def prepare(blocks, ids, b_blocks, occupied):
    rows, block_size = blocks.shape
    return pl.pallas_call(
        prepare_kernel,
        out_shape=(
            jax.ShapeDtypeStruct((rows + TALL, block_size), blocks.dtype),
            jax.ShapeDtypeStruct(b_blocks.shape, b_blocks.dtype),
        ),
        in_specs=[ANY] * 4,
        out_specs=(ANY, ANY),
        scratch_shapes=[
            pltpu.SMEM(ids.shape, jnp.int32),
            pltpu.SMEM(occupied.shape, jnp.int32),
            pltpu.VMEM(b_blocks.shape, b_blocks.dtype),
            pltpu.VMEM((rows + TALL, block_size), blocks.dtype),
            pltpu.SemaphoreType.DMA((6,)),
        ],
        compiler_params=pltpu.CompilerParams(vmem_limit_bytes=60 * 1024 * 1024),
    )(blocks, ids, b_blocks, occupied)


def choose_kernel(owner_ref, keep_ref, chosen_ref, kept_ref):
    layer_count, half_rows = owner_ref.shape
    out_count, block_size = chosen_ref.shape
    width = kept_ref.shape[1]
    col, layer = lax.axis_index("col"), lax.axis_index("layer")
    lane = lax.broadcasted_iota(jnp.int32, (1, width), 1)
    for q in range(out_count):
        half = q % layer_count
        m = half * half_rows + owner_ref[half, (col ^ (q // layer_count)) * layer_count + layer]
        kept = jnp.zeros((1, width), jnp.int32)
        for n in range(width // block_size):
            kept = jnp.where(lane // block_size == n, keep_ref[n, m], kept)
        kept_ref[q : q + 1, :] = kept.astype(jnp.float32)
        chosen_ref[q : q + 1, :] = jnp.full((1, block_size), m, jnp.int32).astype(jnp.float32)


def choose(owner_rows, keep, block_size):
    out_count = owner_rows.shape[1]
    return pl.pallas_call(
        choose_kernel,
        out_shape=(
            jax.ShapeDtypeStruct((out_count, block_size), jnp.float32),
            jax.ShapeDtypeStruct((out_count, keep.shape[0] * block_size), jnp.float32),
        ),
        in_specs=[SMEM] * 2,
        out_specs=[VMEM] * 2,
        compiler_params=LIMIT,
    )(owner_rows, keep)


def pick(slot_count, piece_refs, chosen_ref, queries):
    block_size = chosen_ref.shape[1]
    rows = slot_count * block_size
    listed = [ref[rows : rows + TALL, :].astype(jnp.float32) for ref in piece_refs]
    lines = []
    for q in queries:
        parts = []
        for n, ref in enumerate(piece_refs):
            part = None
            for s in range(slot_count):
                same = (listed[n][s : s + 1, :] == chosen_ref[pl.ds(q, 1), :]).astype(jnp.float32)
                same = jnp.broadcast_to(same, (TALL, block_size)).astype(ref.dtype)
                same = jnp.concatenate([same] * (block_size // TALL), axis=0)
                block = ref[s * block_size : (s + 1) * block_size, :] * same
                part = block if part is None else part + block
            parts.append(part)
        lines.append(jnp.concatenate(parts, axis=1))
    return jnp.concatenate(lines, axis=0)


def early_kernel(slot_count, chosen_ref, slab_ref, twin_ref, *refs):
    *piece_refs, total_ref, last_ref, panels = refs
    steps = len(piece_refs)
    col_count, local_rows, block_size, width = slab_ref.shape
    out_count = total_ref.shape[0]
    layer_count = out_count // col_count
    row, col = lax.axis_index("row"), lax.axis_index("col")
    for flip_col in range(col_count):
        for flip_layer, ref in enumerate((slab_ref, twin_ref)):
            for j in range(local_rows):
                turn = turn_of((col ^ flip_col) * local_rows + j, row, col_count * local_rows)
                panels[turn * layer_count + flip_layer] = ref[flip_col, j]
    for n in range(last_ref.shape[0] // block_size):
        last_ref[n * block_size : (n + 1) * block_size, :] = panels[steps + n]

    def add(at, carry):
        queries = [at * layer_count + n for n in range(layer_count)]
        total = jnp.dot(
            pick(slot_count, piece_refs, chosen_ref, queries),
            panels[:steps].reshape(steps * block_size, width),
            preferred_element_type=jnp.float32,
        )
        for n, q in enumerate(queries):
            total_ref[q] = total[n * block_size : (n + 1) * block_size]
        return carry

    if steps > 16:
        lax.fori_loop(0, col_count, add, 0)
    else:
        for at in range(col_count):
            add(at, 0)


def early(slot_count, late_count, chosen, slabs, twins, pieces):
    block_size, width = slabs.shape[2:]
    steps, kind = len(pieces), slabs.dtype
    return pl.pallas_call(
        functools.partial(early_kernel, slot_count),
        out_shape=(
            jax.ShapeDtypeStruct((chosen.shape[0], block_size, width), jnp.float32),
            jax.ShapeDtypeStruct((late_count * block_size, width), kind),
        ),
        in_specs=[VMEM] * (3 + steps),
        out_specs=[VMEM] * 2,
        scratch_shapes=[pltpu.VMEM((steps + late_count, block_size, width), kind)],
        compiler_params=LIMIT,
    )(chosen, slabs, twins, *pieces)


def late_kernel(slot_count, col_count, chips, total_ref, last_ref, chosen_ref, kept_ref, *refs):
    piece_refs, out_refs = refs[: -len(chips)], refs[-len(chips) :]
    block_size = total_ref.shape[1]
    layer_count = total_ref.shape[0] // col_count
    for at, out_ref in zip(chips, out_refs):
        queries = range(at * layer_count, (at + 1) * layer_count)
        lines = pick(slot_count, piece_refs, chosen_ref, queries)
        total = jnp.dot(lines, last_ref[...], preferred_element_type=jnp.float32)
        for n, q in enumerate(queries):
            part = total[n * block_size : (n + 1) * block_size] + total_ref[q]
            out_ref[n] = (part * kept_ref[q : q + 1, :]).astype(out_ref.dtype)


def late(slot_count, col_count, chips, totals, chosen, kept, pieces):
    total, last = totals
    out_count, block_size, width = total.shape
    shape = jax.ShapeDtypeStruct((out_count // col_count, block_size, width), last.dtype)
    return pl.pallas_call(
        functools.partial(late_kernel, slot_count, col_count, chips),
        out_shape=[shape] * len(chips),
        in_specs=[VMEM] * (4 + len(pieces)),
        out_specs=[VMEM] * len(chips),
        compiler_params=LIMIT,
    )(total, last, chosen, kept, *pieces)


def collect_kernel(*refs):
    *part_refs, out_ref, done = refs
    count, col = part_refs[0].shape[0], lax.axis_index("col")
    copies = []
    for flip_col, ref in enumerate(part_refs[::-1]):
        at = pl.multiple_of((col ^ flip_col) * count, count)
        copies.append(pltpu.make_async_copy(ref, out_ref.at[pl.ds(at, count)], done.at[flip_col]))
    for copy in copies:
        copy.start()
    for copy in copies:
        copy.wait()


def collect(parts):
    count, block_size, width = parts[0].shape
    return pl.pallas_call(
        collect_kernel,
        out_shape=jax.ShapeDtypeStruct((count * len(parts), block_size, width), parts[0].dtype),
        in_specs=[VMEM] * len(parts),
        out_specs=ANY,
        scratch_shapes=[pltpu.SemaphoreType.DMA((len(parts),))],
        compiler_params=LIMIT,
    )(*parts[::-1])


def swap(value, axis, by):
    return lax.ppermute(value, axis, [(i, i ^ by) for i in range(lax.axis_size(axis))])


def shards(a_blocks, a_rows, b_blocks, b_occupied, keep, owner_rows):
    local_rows, _, block_size, width = b_blocks.shape
    slot_count = a_rows.shape[3]
    row_count, col_count, layer_count = (lax.axis_size(name) for name in ("row", "col", "layer"))
    ring = list(range(0, row_count, 2)) + list(range(row_count - 1, 0, -2))
    turns = [(n // 2 + 1) * (1 if n % 2 == 0 else -1) for n in range(row_count - 1)]
    turns = [0] + sorted(turns, key=abs)

    own, masked = prepare(
        a_blocks.reshape(slot_count * block_size, block_size),
        a_rows.reshape(1, slot_count),
        b_blocks.reshape(local_rows, block_size, width),
        b_occupied.reshape(local_rows, -1),
    )
    chosen, kept = choose(owner_rows[0], keep.T, block_size)
    slabs = [masked] + [swap(masked, "col", by) for by in range(1, col_count)]
    chosen, kept, *slabs = lax.optimization_barrier((chosen, kept, *slabs))
    slabs = jnp.stack(slabs)
    twins = swap(slabs, "layer", 1)
    held = {0: own}
    for turn in turns[1:]:
        step = 1 if turn > 0 else -1
        held[turn] = lax.ppermute(
            held[turn - step], "row", [(name, ring[(at + step) % row_count]) for at, name in enumerate(ring)]
        )
    split = row_count - 1
    pieces = [one for turn in turns for one in (held[turn], swap(held[turn], "layer", 1))]
    steps = split * layer_count
    totals = early(slot_count, len(pieces) - steps, chosen, slabs, twins, pieces[:steps])
    far, final = col_count - 1, pieces[split * layer_count :]
    parts = list(late(slot_count, col_count, (far,), totals, chosen, kept, final))
    kept, parts[0] = lax.optimization_barrier((kept, parts[0]))
    parts = list(late(slot_count, col_count, tuple(range(far)), totals, chosen, kept, final)) + parts
    for by in range(far, 0, -1):
        parts[by] = swap(parts[by], "col", by)
    return collect(parts)[None]


def solution(mesh):
    return jax.shard_map(
        shards,
        mesh=mesh,
        in_specs=(
            P(("grp", "row"), "layer", "col", None, None, None),
            P(("grp", "row"), "layer", "col", None),
            P(("grp", "col"), "layer", None, "row"),
            P(("grp", "col"), "layer", "row"),
            P(("grp", "col"), "row"),
            P(("grp", "col"), None, None),
        ),
        out_specs=P(("grp", "col", "layer"), None, None, "row"),
        check_vma=False,
    )
```

```python
import functools

import jax
import jax.numpy as jnp
from jax import lax
from jax.experimental import pallas as pl
from jax.experimental.pallas import tpu as pltpu
from jax.sharding import PartitionSpec as P

SMEM = pl.BlockSpec(memory_space=pltpu.SMEM)
VMEM = pl.BlockSpec(memory_space=pltpu.VMEM)
LIMIT = pltpu.CompilerParams(vmem_limit_bytes=48 * 1024 * 1024)
ANY = pl.BlockSpec(memory_space=pl.ANY)
TALL = 16


def turn_of(source, here, row_count):
    spots = [jnp.where(n % 2 == 1, n // 2 + 1, jnp.where(n == 0, 0, row_count - n // 2)) for n in (here, source)]
    ahead = (spots[1] - spots[0]) & (row_count - 1)
    return jnp.where(ahead == 0, 0, jnp.where(ahead <= row_count // 2, 2 * ahead - 1, 2 * (row_count - ahead)))


def prepare_kernel(a_ref, ids_ref, b_ref, occupied_ref, piece_ref, masked_ref, ids, occupied, panel, piece, done):
    rows, slot_count = a_ref.shape[0], ids.shape[1]
    local_rows, block_size, width = panel.shape
    copies = [
        pltpu.make_async_copy(ids_ref, ids, done.at[0]),
        pltpu.make_async_copy(occupied_ref, occupied, done.at[1]),
        pltpu.make_async_copy(b_ref, panel, done.at[2]),
        pltpu.make_async_copy(a_ref, piece.at[pl.ds(0, rows)], done.at[3]),
    ]
    for copy in copies:
        copy.start()
    copies[0].wait()
    line = lax.broadcasted_iota(jnp.int32, (TALL, block_size), 0)
    listed = jnp.full(line.shape, -1, jnp.int32)
    for s in range(slot_count):
        listed = jnp.where(line == s, ids[0, s], listed)
    piece[rows:, :] = listed.astype(jnp.float32).astype(piece.dtype)
    copies[3].wait()
    piece_out = pltpu.make_async_copy(piece, piece_ref, done.at[4])
    piece_out.start()
    copies[1].wait()
    copies[2].wait()
    lane = lax.broadcasted_iota(jnp.int32, (1, width), 1)
    for j in range(local_rows):
        kept = jnp.zeros((1, width), jnp.int32)
        for n in range(width // block_size):
            kept = jnp.where(lane // block_size == n, occupied[j, n], kept)
        panel[j] = panel[j] * kept.astype(jnp.float32).astype(panel.dtype)
    panel_out = pltpu.make_async_copy(panel, masked_ref, done.at[5])
    panel_out.start()
    piece_out.wait()
    panel_out.wait()


def prepare(blocks, ids, b_blocks, occupied):
    rows, block_size = blocks.shape
    return pl.pallas_call(
        prepare_kernel,
        out_shape=(
            jax.ShapeDtypeStruct((rows + TALL, block_size), blocks.dtype),
            jax.ShapeDtypeStruct(b_blocks.shape, b_blocks.dtype),
        ),
        in_specs=[ANY] * 4,
        out_specs=(ANY, ANY),
        scratch_shapes=[
            pltpu.SMEM(ids.shape, jnp.int32),
            pltpu.SMEM(occupied.shape, jnp.int32),
            pltpu.VMEM(b_blocks.shape, b_blocks.dtype),
            pltpu.VMEM((rows + TALL, block_size), blocks.dtype),
            pltpu.SemaphoreType.DMA((6,)),
        ],
        compiler_params=pltpu.CompilerParams(vmem_limit_bytes=60 * 1024 * 1024),
    )(blocks, ids, b_blocks, occupied)


def choose_kernel(owner_ref, keep_ref, chosen_ref, kept_ref):
    layer_count, half_rows = owner_ref.shape
    out_count, block_size = chosen_ref.shape
    width = kept_ref.shape[1]
    col, layer = lax.axis_index("col"), lax.axis_index("layer")
    lane = lax.broadcasted_iota(jnp.int32, (1, width), 1)
    for q in range(out_count):
        half = q % layer_count
        m = half * half_rows + owner_ref[half, (col ^ (q // layer_count)) * layer_count + layer]
        kept = jnp.zeros((1, width), jnp.int32)
        for n in range(width // block_size):
            kept = jnp.where(lane // block_size == n, keep_ref[n, m], kept)
        kept_ref[q : q + 1, :] = kept.astype(jnp.float32)
        chosen_ref[q : q + 1, :] = jnp.full((1, block_size), m, jnp.int32).astype(jnp.float32)


def choose(owner_rows, keep, block_size):
    out_count = owner_rows.shape[1]
    return pl.pallas_call(
        choose_kernel,
        out_shape=(
            jax.ShapeDtypeStruct((out_count, block_size), jnp.float32),
            jax.ShapeDtypeStruct((out_count, keep.shape[0] * block_size), jnp.float32),
        ),
        in_specs=[SMEM] * 2,
        out_specs=[VMEM] * 2,
        compiler_params=LIMIT,
    )(owner_rows, keep)


def pick(slot_count, piece_refs, chosen_ref, queries):
    block_size = chosen_ref.shape[1]
    rows = slot_count * block_size
    listed = [ref[rows : rows + TALL, :].astype(jnp.float32) for ref in piece_refs]
    lines = []
    for q in queries:
        parts = []
        for n, ref in enumerate(piece_refs):
            part = None
            for s in range(slot_count):
                same = (listed[n][s : s + 1, :] == chosen_ref[pl.ds(q, 1), :]).astype(jnp.float32)
                same = jnp.broadcast_to(same, (TALL, block_size)).astype(ref.dtype)
                same = jnp.concatenate([same] * (block_size // TALL), axis=0)
                block = ref[s * block_size : (s + 1) * block_size, :] * same
                part = block if part is None else part + block
            parts.append(part)
        lines.append(jnp.concatenate(parts, axis=1))
    return jnp.concatenate(lines, axis=0)


def early_kernel(slot_count, chosen_ref, slab_ref, twin_ref, *refs):
    *piece_refs, total_ref, last_ref, panels = refs
    steps = len(piece_refs)
    col_count, local_rows, block_size, width = slab_ref.shape
    out_count = total_ref.shape[0]
    layer_count = out_count // col_count
    row, col = lax.axis_index("row"), lax.axis_index("col")
    for flip_col in range(col_count):
        for flip_layer, ref in enumerate((slab_ref, twin_ref)):
            for j in range(local_rows):
                turn = turn_of((col ^ flip_col) * local_rows + j, row, col_count * local_rows)
                panels[turn * layer_count + flip_layer] = ref[flip_col, j]
    for n in range(last_ref.shape[0] // block_size):
        last_ref[n * block_size : (n + 1) * block_size, :] = panels[steps + n]

    def add(at, carry):
        queries = [at * layer_count + n for n in range(layer_count)]
        total = jnp.dot(
            pick(slot_count, piece_refs, chosen_ref, queries),
            panels[:steps].reshape(steps * block_size, width),
            preferred_element_type=jnp.float32,
        )
        for n, q in enumerate(queries):
            total_ref[q] = total[n * block_size : (n + 1) * block_size]
        return carry

    if steps > 16:
        lax.fori_loop(0, col_count, add, 0)
    else:
        for at in range(col_count):
            add(at, 0)


def early(slot_count, late_count, chosen, slabs, twins, pieces):
    block_size, width = slabs.shape[2:]
    steps, kind = len(pieces), slabs.dtype
    return pl.pallas_call(
        functools.partial(early_kernel, slot_count),
        out_shape=(
            jax.ShapeDtypeStruct((chosen.shape[0], block_size, width), jnp.float32),
            jax.ShapeDtypeStruct((late_count * block_size, width), kind),
        ),
        in_specs=[VMEM] * (3 + steps),
        out_specs=[VMEM] * 2,
        scratch_shapes=[pltpu.VMEM((steps + late_count, block_size, width), kind)],
        compiler_params=LIMIT,
    )(chosen, slabs, twins, *pieces)


def late_kernel(slot_count, col_count, chips, total_ref, last_ref, chosen_ref, kept_ref, *refs):
    piece_refs, out_refs = refs[: -len(chips)], refs[-len(chips) :]
    block_size = total_ref.shape[1]
    layer_count = total_ref.shape[0] // col_count
    for at, out_ref in zip(chips, out_refs):
        queries = range(at * layer_count, (at + 1) * layer_count)
        lines = pick(slot_count, piece_refs, chosen_ref, queries)
        total = jnp.dot(lines, last_ref[...], preferred_element_type=jnp.float32)
        for n, q in enumerate(queries):
            part = total[n * block_size : (n + 1) * block_size] + total_ref[q]
            out_ref[n] = (part * kept_ref[q : q + 1, :]).astype(out_ref.dtype)


def late(slot_count, col_count, chips, totals, chosen, kept, pieces):
    total, last = totals
    out_count, block_size, width = total.shape
    shape = jax.ShapeDtypeStruct((out_count // col_count, block_size, width), last.dtype)
    return pl.pallas_call(
        functools.partial(late_kernel, slot_count, col_count, chips),
        out_shape=[shape] * len(chips),
        in_specs=[VMEM] * (4 + len(pieces)),
        out_specs=[VMEM] * len(chips),
        compiler_params=LIMIT,
    )(total, last, chosen, kept, *pieces)


def collect_kernel(*refs):
    *part_refs, out_ref, done = refs
    count, col = part_refs[0].shape[0], lax.axis_index("col")
    copies = []
    for flip_col, ref in enumerate(part_refs[::-1]):
        at = pl.multiple_of((col ^ flip_col) * count, count)
        copies.append(pltpu.make_async_copy(ref, out_ref.at[pl.ds(at, count)], done.at[flip_col]))
    for copy in copies:
        copy.start()
    for copy in copies:
        copy.wait()


def collect(parts):
    count, block_size, width = parts[0].shape
    return pl.pallas_call(
        collect_kernel,
        out_shape=jax.ShapeDtypeStruct((count * len(parts), block_size, width), parts[0].dtype),
        in_specs=[VMEM] * len(parts),
        out_specs=ANY,
        scratch_shapes=[pltpu.SemaphoreType.DMA((len(parts),))],
        compiler_params=LIMIT,
    )(*parts[::-1])


def swap(value, axis, by):
    return lax.ppermute(value, axis, [(i, i ^ by) for i in range(lax.axis_size(axis))])


def shards(a_blocks, a_rows, b_blocks, b_occupied, keep, owner_rows):
    local_rows, _, block_size, width = b_blocks.shape
    slot_count = a_rows.shape[3]
    row_count, col_count, layer_count = (lax.axis_size(name) for name in ("row", "col", "layer"))
    ring = list(range(0, row_count, 2)) + list(range(row_count - 1, 0, -2))
    turns = [(n // 2 + 1) * (1 if n % 2 == 0 else -1) for n in range(row_count - 1)]
    turns = [0] + sorted(turns, key=abs)

    own, masked = prepare(
        a_blocks.reshape(slot_count * block_size, block_size),
        a_rows.reshape(1, slot_count),
        b_blocks.reshape(local_rows, block_size, width),
        b_occupied.reshape(local_rows, -1),
    )
    chosen, kept = choose(owner_rows[0], keep.T, block_size)
    slabs = [masked] + [swap(masked, "col", by) for by in range(1, col_count)]
    chosen, kept, *slabs = lax.optimization_barrier((chosen, kept, *slabs))
    slabs = jnp.stack(slabs)
    twins = swap(slabs, "layer", 1)
    held = {0: own}
    for turn in turns[1:]:
        step = 1 if turn > 0 else -1
        held[turn] = lax.ppermute(
            held[turn - step], "row", [(name, ring[(at + step) % row_count]) for at, name in enumerate(ring)]
        )
    split = row_count - 2
    pieces = [one for turn in turns for one in (held[turn], swap(held[turn], "layer", 1))]
    steps = split * layer_count
    totals = early(slot_count, len(pieces) - steps, chosen, slabs, twins, pieces[:steps])
    far, final = col_count - 1, pieces[split * layer_count :]
    parts = list(late(slot_count, col_count, (far,), totals, chosen, kept, final))
    kept, parts[0] = lax.optimization_barrier((kept, parts[0]))
    parts = list(late(slot_count, col_count, tuple(range(far)), totals, chosen, kept, final)) + parts
    for by in range(far, 0, -1):
        parts[by] = swap(parts[by], "col", by)
    return collect(parts)[None]


def solution(mesh):
    return jax.shard_map(
        shards,
        mesh=mesh,
        in_specs=(
            P(("grp", "row"), "layer", "col", None, None, None),
            P(("grp", "row"), "layer", "col", None),
            P(("grp", "col"), "layer", None, "row"),
            P(("grp", "col"), "layer", "row"),
            P(("grp", "col"), "row"),
            P(("grp", "col"), None, None),
        ),
        out_specs=P(("grp", "col", "layer"), None, None, "row"),
        check_vma=False,
    )
```
